128 devices in a mesh: owner: 32 (over y, z, core), group: 4 (over x).
Axes of the slice: x: 4, y: 4, z: 4, core: 2. Of those that a mesh axis runs over, the one named last changes fastest.
Arguments:
- right_side: bfloat16 [64, 2, 4, 4, 128, 128], P('owner', None, 'group'), may hold values from -6 to 6
- hops: bfloat16 [8, 64, 2, 4, 4, 128, 128], P(None, 'owner'), may hold values from -0.09375 to 0.09375
- diag_inverse: bfloat16 [64, 2, 4, 4, 128, 128], P('owner'), may hold values from -0.16 to 2, as said below
- prolongator: bfloat16 [64, 2, 4, 4, 128, 384], P('owner', None, 'group'), may hold values from -0.5 to 0.5
Outputs:
- coarse_solution: bfloat16 [64, 2, 4, 4, 128, 128], P('owner', None, 'group')
- fine_correction: bfloat16 [64, 2, 4, 4, 128, 384], P('owner', None, 'group')
The draws below stay inside these ranges and needn't reach their ends.
Inputs may be any that keep to these rules, and one draw needn't show every extreme that they name: `diag_inverse`: each site's block has its diagonal entries between 0.25 and 2 and off-diagonal entries of at most 0.16 in magnitude.
All inputs are finite; a program needn't handle non-finite values.
Results may differ from the reference program's by a relative error of at most 0.0067.
Values may be sent and summed in bfloat16 or wider, within the bound.
A program may use at most 128 MiB of HBM per device.

```python
import jax
import jax.numpy as jnp

C = 128
NRHS = 128
SX = 4
SY = 4
SZ = 2
ITERS = 4
NT = 64
FINE = 384


def draw_diag_inverse(key, part):
    first_key, second_key = jax.random.split(key)
    diagonal = jax.random.uniform(first_key, (NT, SZ, SY, SX, C), jnp.float32, 0.5, 1.5)
    offdiag = jnp.clip(jax.random.normal(second_key, (NT, SZ, SY, SX, C, C), jnp.float32), -4.0, 4.0) * 0.039
    identity = jnp.eye(C, dtype=jnp.float32)
    return (offdiag * (1.0 - identity) + identity * diagonal[..., None]).astype(jnp.bfloat16)


def block_levels(stream_key, shape, cuts, least, top_value):
    level, own = 1.0, jax.random.fold_in(stream_key, 6)
    for position, parts in cuts:
        heights = jnp.exp(jax.random.uniform(jax.random.fold_in(own, position), (parts,), jnp.float32, least / len(cuts), top_value / len(cuts)))
        level = level * jnp.repeat(heights, shape[position] // parts).reshape([-1 if axis == position else 1 for axis in range(len(shape))])
    return level


def noise(stream_key, shape, scale, most, pieces=(), kind=jnp.bfloat16):
    level = block_levels(stream_key, shape, pieces, -0.22, 0.18) if pieces else 1.0
    values = jax.random.normal(stream_key, shape, jnp.float32) * scale * level
    return jnp.minimum(jnp.maximum(values, -most), most).astype(kind)


def setup_inputs(seed: int = 0) -> dict:
    seeds = jax.random.split(jax.random.key(seed), 5)
    right_side = noise(seeds[0], (NT, SZ, SY, SX, NRHS, C), 1.0, 6.0, ((0, 32), (2, 4)))
    hops = noise(seeds[1], (8, NT, SZ, SY, SX, C, C), (32 * C) ** -0.5, 0.09375, ((1, 32),))
    diag_inverse = draw_diag_inverse(jax.random.fold_in(seeds[4], 71), 0)
    prolongator = noise(seeds[3], (NT, SZ, SY, SX, C, FINE), C ** -0.5, 0.5, ((0, 32), (2, 4)))
    return dict(right_side=right_side, hops=hops, diag_inverse=diag_inverse, prolongator=prolongator)


def shifted(field):
    return [jnp.roll(field, -1, 3), jnp.roll(field, 1, 3),
            jnp.roll(field, -1, 2), jnp.roll(field, 1, 2),
            jnp.roll(field, -1, 1), jnp.roll(field, 1, 1),
            jnp.roll(field, -1, 0), jnp.roll(field, 1, 0)]


def hop_total(hops, field):
    total = jnp.zeros(field.shape, jnp.float32)
    for direction, neighbour in enumerate(shifted(field)):
        total = total + jnp.einsum('tzyxrd,tzyxcd->tzyxrc', neighbour.astype(jnp.float32), hops[direction].astype(jnp.float32))
    return total


def apply_inverse(inverse, field):
    return jnp.einsum('tzyxcd,tzyxrd->tzyxrc', inverse.astype(jnp.float32), field.astype(jnp.float32)).astype(jnp.bfloat16)


def reference(right_side, hops, diag_inverse, prolongator):
    iterate = apply_inverse(diag_inverse, right_side)
    for iteration in range(ITERS - 1):
        remainder = (right_side.astype(jnp.float32) - hop_total(hops, iterate)).astype(jnp.bfloat16)
        iterate = apply_inverse(diag_inverse, remainder)
    fine_correction = jnp.einsum('tzyxrc,tzyxcf->tzyxrf', iterate.astype(jnp.float32), prolongator.astype(jnp.float32)).astype(jnp.bfloat16)
    return iterate, fine_correction
```

```python
import functools

import jax
import jax.numpy as jnp
from jax import lax
from jax.experimental import pallas as pl
from jax.experimental.pallas import tpu as pltpu
from jax.sharding import PartitionSpec as P

MESH = pl.DeviceIdType.MESH
ITERS = 4
C = 128
PART = 32
DIRS = 7
F32 = jnp.float32
BF16 = jnp.bfloat16


def dot(left, right):
    return lax.dot_general(
        left, right, (((1,), (0,)), ((), ())), preferred_element_type=F32
    )


def ring(step):
    return step + step // 2 - 2 * (step // 3)


def ring_of(step):
    return step + lax.div(step, 2) - 2 * lax.div(step, 3)


def kernel(
    b_hbm, h_hbm, d_hbm, p_hbm, c_hbm, f_hbm,
    hs, ht, ds, rhs, field, last, acc, gathered, pro, fine,
    h_sem, d_sem, p_sem, b_sem, c_sem, f_sem,
    in_send, in_recv, halo_send, halo_recv, out_send, out_recv,
):
    g = lax.axis_index("group")
    o = lax.axis_index("owner")
    before, after = lax.rem(o + 31, 32), lax.rem(o + 1, 32)

    def slab(j):
        return lax.rem(g + ring_of(j), 4)

    def part(index):
        return pl.ds(pl.multiple_of(index * PART, PART), PART)

    d_load = pltpu.make_async_copy(d_hbm, ds, d_sem)
    d_load.start()
    b_load = pltpu.make_async_copy(b_hbm.at[:, :, 0, :, part(g), :], rhs.at[:, :, g], b_sem)
    b_load.start()

    def h_load(j, t, z):
        y = slab(j)
        return pltpu.make_async_copy(
            h_hbm.at[:, t, z, y], hs.at[:, t, z, y], h_sem.at[j, t, z]
        )

    def start_loads(j, carry):
        for t in range(2):
            for z in range(2):
                h_load(j, t, z).start()
        return carry

    lax.fori_loop(0, 4, start_loads, 0)
    p_load = pltpu.make_async_copy(p_hbm.at[:, :, 0], pro, p_sem)
    p_load.start()

    barrier = pltpu.get_barrier_semaphore()
    for k in (1, 2, 3):
        pl.semaphore_signal(
            barrier, inc=1, device_id={"group": lax.rem(g + k, 4)}, device_id_type=MESH
        )
    for neighbour in (before, after):
        pl.semaphore_signal(
            barrier, inc=1, device_id={"owner": neighbour}, device_id_type=MESH
        )
    pl.semaphore_wait(barrier, 5)

    opposite = {1: 2, 2: 1, 3: 3}

    def in_copy(j):
        peer = lax.rem(g + ring(j), 4)
        return pltpu.make_async_remote_copy(
            src_ref=b_hbm.at[:, :, 0, :, part(peer), :],
            dst_ref=rhs.at[:, :, g],
            send_sem=in_send.at[j],
            recv_sem=in_recv.at[opposite[j]],
            device_id={"group": peer},
            device_id_type=MESH,
        )

    def in_arrival(j):
        peer = lax.rem(g + ring(j), 4)
        return pltpu.make_async_remote_copy(
            src_ref=b_hbm.at[:, :, 0, :, part(peer), :],
            dst_ref=rhs.at[:, :, peer],
            send_sem=in_send.at[j],
            recv_sem=in_recv.at[j],
            device_id={"group": peer},
            device_id_type=MESH,
        )

    for j in (3, 1, 2):
        in_copy(j).start()

    def halo_copy(it, j, side):
        y = slab(j)
        return pltpu.make_async_remote_copy(
            src_ref=field.at[it, 2 - side, :, y],
            dst_ref=field.at[it, 3 * side, :, y],
            send_sem=halo_send.at[it, j, side],
            recv_sem=halo_recv.at[it, j, side],
            device_id={"owner": before if side else after},
            device_id_type=MESH,
        )

    def send_halo(it, j):
        for side in range(2):
            halo_copy(it, j, side).start()

    def wait_halo(it, j):
        for side in range(2):
            halo_copy(it, j, side).wait_recv()

    sites = [(t, z, x) for t in range(2) for z in range(2) for x in range(4)]

    def transpose_slab(j, carry):
        y = slab(j)
        for t in range(2):
            for z in range(2):
                h_load(j, t, z).wait()
                for x in range(4):
                    inner, outer = (6, 7) if t == 0 else (7, 6)
                    blocks = [hs[k, t, z, y, x] for k in range(4)]
                    blocks.append(hs[4, t, z, y, x] + hs[5, t, z, y, x])
                    blocks.append(hs[inner, t, z, y, x])
                    blocks.append(hs[outer, t, z, y, x])
                    for k, block in enumerate(blocks):
                        ht[t, z, y, x, k * C : (k + 1) * C, :] = block.T
                    ds[t, z, y, x] = ds[t, z, y, x].T
        return carry

    def first(j):
        y = slab(j)
        for t, z, x in sites:
            field[0, t + 1, z, y, x] = dot(rhs[t, z, y, x], ds[t, z, y, x]).astype(BF16)
        send_halo(0, j)

    def interior(it, j):
        y = slab(j)
        up, down = lax.rem(y + 1, 4), lax.rem(y + 3, 4)
        for q, (t, z, x) in enumerate(sites):
            near = jnp.concatenate(
                [
                    field[it, t + 1, z, y, (x + 1) % 4],
                    field[it, t + 1, z, y, (x + 3) % 4],
                    field[it, t + 1, z, up, x],
                    field[it, t + 1, z, down, x],
                    field[it, t + 1, 1 - z, y, x],
                    field[it, 2 - t, z, y, x],
                ],
                axis=1,
            )
            total = dot(near, ht[t, z, y, x, : 6 * C, :])
            acc[q] = rhs[t, z, y, x].astype(F32) - total

    def finish(it, j, store):
        y = slab(j)
        remainders = [
            (acc[q] - dot(field[it, 3 * t, z, y, x], ht[t, z, y, x, 6 * C :, :])).astype(BF16)
            for q, (t, z, x) in enumerate(sites)
        ]
        for remainder, (t, z, x) in zip(remainders, sites):
            store(t, z, y, x, dot(remainder, ds[t, z, y, x]).astype(BF16))

    d_load.wait()
    transpose_slab(0, 0)
    b_load.wait()
    first(0)
    lax.fori_loop(1, 4, transpose_slab, 0)
    for j in range(1, 4):
        in_arrival(j).wait_recv()
        first(j)

    interior(0, 0)
    for it in range(ITERS - 2):

        def store(t, z, y, x, value, it=it):
            field[it + 1, t + 1, z, y, x] = value

        def step(j, carry, it=it, store=store):
            wait_halo(it, j)
            finish(it, j, store)
            send_halo(it + 1, j)
            lax.cond(j < 3, lambda: interior(it, j + 1), lambda: interior(it + 1, 0))
            return carry

        lax.fori_loop(0, 4, step, 0)

    def out_copy(j):
        peer = slab(j)
        return pltpu.make_async_remote_copy(
            src_ref=last.at[:, :, peer],
            dst_ref=gathered.at[:, :, :, part(g), :],
            send_sem=out_send.at[j],
            recv_sem=out_recv.at[j],
            device_id={"group": peer},
            device_id_type=MESH,
        )

    def store_last(t, z, y, x, value):
        last[t, z, y, x] = value

    def store_own(t, z, y, x, value):
        gathered[t, z, x, part(g), :] = value

    it = ITERS - 2
    wait_halo(it, 0)
    finish(it, 0, store_own)

    def last_step(j, carry):
        interior(it, j)
        wait_halo(it, j)
        finish(it, j, store_last)
        out_copy(j).start()
        return carry

    lax.fori_loop(1, 4, last_step, 0)

    p_load.wait()
    for j in range(1, 4):
        out_copy(j).wait_recv()
    c_store = pltpu.make_async_copy(gathered, c_hbm.at[:, :, 0], c_sem)
    c_store.start()

    def f_store(t, z):
        return pltpu.make_async_copy(fine.at[t, z], f_hbm.at[t, z, 0], f_sem.at[t, z])

    for t in range(2):
        for z in range(2):
            for x in range(4):
                fine[t, z, x] = dot(gathered[t, z, x], pro[t, z, x]).astype(BF16)
            f_store(t, z).start()

    c_store.wait()
    for t in range(2):
        for z in range(2):
            f_store(t, z).wait()
    for j in range(1, 4):
        in_copy(j).wait_send()
        out_copy(j).wait_send()

    def drain(j, carry):
        for k in range(ITERS - 1):
            for side in range(2):
                halo_copy(k, j, side).wait_send()
        return carry

    lax.fori_loop(0, 4, drain, 0)


def on_device(right_side, hops, diag_inverse, prolongator):
    vmem, dma = pltpu.VMEM, pltpu.SemaphoreType.DMA
    fine_width = prolongator.shape[-1]
    return pl.pallas_call(
        kernel,
        out_shape=(
            jax.ShapeDtypeStruct(right_side.shape, BF16),
            jax.ShapeDtypeStruct(prolongator.shape, BF16),
        ),
        in_specs=[pl.BlockSpec(memory_space=pl.ANY)] * 4,
        out_specs=(pl.BlockSpec(memory_space=pl.ANY),) * 2,
        scratch_shapes=[
            vmem((8, 2, 2, 4, 4, C, C), BF16),
            vmem((2, 2, 4, 4, DIRS * C, C), BF16),
            vmem((2, 2, 4, 4, C, C), BF16),
            vmem((2, 2, 4, 4, PART, C), BF16),
            vmem((ITERS - 1, 4, 2, 4, 4, PART, C), BF16),
            vmem((2, 2, 4, 4, PART, C), BF16),
            vmem((16, PART, C), F32),
            vmem((2, 2, 4, C, C), BF16),
            vmem((2, 2, 4, C, fine_width), BF16),
            vmem((2, 2, 4, C, fine_width), BF16),
            dma((4, 2, 2)),
            dma,
            dma,
            dma,
            dma,
            dma((2, 2)),
            dma((4,)),
            dma((4,)),
            dma((ITERS - 1, 4, 2)),
            dma((ITERS - 1, 4, 2)),
            dma((4,)),
            dma((4,)),
        ],
        compiler_params=pltpu.CompilerParams(
            collective_id=0, has_side_effects=True, vmem_limit_bytes=60 * 1024 * 1024
        ),
        cost_estimate=pl.CostEstimate(
            flops=2 * 64 * 28 * C * C * PART, bytes_accessed=24 * 1024 * 1024, transcendentals=0
        ),
    )(right_side, hops, diag_inverse, prolongator)


def solution(mesh):
    placed = (
        P("owner", None, "group", None, None, None),
        P(None, "owner", None, None, None, None, None),
        P("owner", None, None, None, None, None),
        P("owner", None, "group", None, None, None),
    )
    return jax.shard_map(
        on_device,
        mesh=mesh,
        in_specs=placed,
        out_specs=(
            P("owner", None, "group", None, None, None),
            P("owner", None, "group", None, None, None),
        ),
        check_vma=False,
    )
```

```python
import functools

import jax
import jax.numpy as jnp
from jax import lax
from jax.experimental import pallas as pl
from jax.experimental.pallas import tpu as pltpu
from jax.sharding import PartitionSpec as P

MESH = pl.DeviceIdType.MESH
ITERS = 4
C = 128
PART = 32
DIRS = 7
OFF, IN = 0, 1
VMEM_LIMIT = 56 * 1024 * 1024
F32 = jnp.float32
BF16 = jnp.bfloat16


def dot(left, right):
    return lax.dot_general(
        left, right, (((1,), (0,)), ((), ())), preferred_element_type=F32
    )


def offset_of(step):
    return lax.rem(2 + 3 * step + 3 * lax.div(step, 2) + 2 * lax.div(step, 3), 4)


MIRROR = (0, 2, 1)


def kernel(
    b_hbm, h_hbm, d_hbm, p_hbm, gathered, fine, pro_off,
    hs, ht, ds, rhs, field, last, acc, pro_in,
    h_sem, d_sem, p_sem, b_sem,
    in_send, in_recv, halo_send, halo_recv, out_send, out_recv,
):
    g = lax.axis_index("group")
    o = lax.axis_index("owner")
    core = lax.rem(o, 2)
    times = (core, 1 - core)

    def slab(j):
        return lax.rem(g + offset_of(j), 4)

    def part(index):
        return pl.ds(pl.multiple_of(index * PART, PART), PART)

    d_load = pltpu.make_async_copy(d_hbm, ds, d_sem)
    d_load.start()
    b_load = pltpu.make_async_copy(b_hbm.at[:, :, 0, :, part(g), :], rhs.at[:, :, g], b_sem)
    b_load.start()

    def h_load(kind, j, z):
        t, y = times[kind], slab(j)
        return pltpu.make_async_copy(
            h_hbm.at[:, t, z, y], hs.at[:, t, z, y], h_sem.at[kind, j, z]
        )

    for kind in (OFF, IN):

        def start_loads(j, carry, kind=kind):
            for z in range(2):
                h_load(kind, j, z).start()
            return carry

        lax.fori_loop(0, 4, start_loads, 0)
    p_loads = [
        pltpu.make_async_copy(p_hbm.at[times[IN], :, 0], pro_in, p_sem.at[IN]),
        pltpu.make_async_copy(p_hbm.at[times[OFF], :, 0], pro_off, p_sem.at[OFF]),
    ]
    for load in p_loads:
        load.start()

    barrier = pltpu.get_barrier_semaphore()
    for k in (1, 2, 3):
        pl.semaphore_signal(
            barrier, inc=1, device_id={"group": lax.rem(g + k, 4)}, device_id_type=MESH
        )
    for k in (1, 31):
        pl.semaphore_signal(
            barrier, inc=1, device_id={"owner": lax.rem(o + k, 32)}, device_id_type=MESH
        )

    def in_copy(kind, j, arrives=False):
        peer, t = slab(j), times[kind]
        return pltpu.make_async_remote_copy(
            src_ref=b_hbm.at[t, :, 0, :, part(peer), :],
            dst_ref=rhs.at[t, :, peer if arrives else g],
            send_sem=in_send.at[kind, j],
            recv_sem=in_recv.at[kind, j if arrives else MIRROR[j]],
            device_id={"group": peer},
            device_id_type=MESH,
        )

    def halo_copy(kind, it, j, arrives=False):
        t, y = times[kind], slab(j)
        return pltpu.make_async_remote_copy(
            src_ref=field.at[it, t + 1, :, y],
            dst_ref=field.at[it, 3 * t if arrives else 3 - 3 * t, :, y],
            send_sem=halo_send.at[kind, it, j],
            recv_sem=halo_recv.at[kind, it, j],
            device_id={"owner": lax.rem(o + 31 + 2 * t, 32)},
            device_id_type=MESH,
        )

    sites = [(z, x) for z in range(2) for x in range(4)]

    def transpose_slab(kind, j):
        t, y = times[kind], slab(j)
        inner, outer = 6 + t, 7 - t
        for z in range(2):
            h_load(kind, j, z).wait()
            for x in range(4):
                blocks = [hs[k, t, z, y, x] for k in range(4)]
                blocks.append(hs[4, t, z, y, x] + hs[5, t, z, y, x])
                blocks.append(hs[inner, t, z, y, x])
                blocks.append(hs[outer, t, z, y, x])
                for k, block in enumerate(blocks):
                    ht[t, z, y, x, k * C : (k + 1) * C, :] = block.T

    def transpose_inverse(kind, j):
        t, y = times[kind], slab(j)
        for z, x in sites:
            ds[t, z, y, x] = ds[t, z, y, x].T

    def first(kind, j):
        t, y = times[kind], slab(j)
        for z, x in sites:
            field[0, t + 1, z, y, x] = dot(rhs[t, z, y, x], ds[t, z, y, x]).astype(BF16)
        halo_copy(kind, 0, j).start()

    def near(it, t, z, y, x):
        return [
            field[it, t + 1, z, y, (x + 1) % 4],
            field[it, t + 1, z, y, (x + 3) % 4],
            field[it, t + 1, z, lax.rem(y + 1, 4), x],
            field[it, t + 1, z, lax.rem(y + 3, 4), x],
            field[it, t + 1, 1 - z, y, x],
            field[it, 2 - t, z, y, x],
        ]

    def interior(it, pair):
        t = times[OFF]
        for j in (2 * pair, 2 * pair + 1):
            y = slab(j)
            for q, (z, x) in enumerate(sites):
                total = dot(
                    jnp.concatenate(near(it, t, z, y, x), axis=1), ht[t, z, y, x, : 6 * C, :]
                )
                acc[j, q] = rhs[t, z, y, x].astype(F32) - total

    def finish_off(it, j, store):
        t, y = times[OFF], slab(j)
        halo_copy(OFF, it, j, True).wait_recv()
        remainders = [
            acc[j, q] - dot(field[it, 3 * t, z, y, x], ht[t, z, y, x, 6 * C :, :])
            for q, (z, x) in enumerate(sites)
        ]
        for remainder, (z, x) in zip(remainders, sites):
            value = dot(remainder.astype(BF16), ds[t, z, y, x]).astype(BF16)
            store(t, z, y, x, value)

    def finish_in(it, steps, stores):
        t = times[IN]
        for j in steps:
            halo_copy(IN, it, j, True).wait_recv()
        places = [(k, slab(j), z, x) for k, j in enumerate(steps) for z, x in sites]
        remainders = [
            rhs[t, z, y, x].astype(F32)
            - dot(
                jnp.concatenate(near(it, t, z, y, x) + [field[it, 3 * t, z, y, x]], axis=1),
                ht[t, z, y, x],
            )
            for k, y, z, x in places
        ]
        for remainder, (k, y, z, x) in zip(remainders, places):
            value = dot(remainder.astype(BF16), ds[t, z, y, x]).astype(BF16)
            stores[k](t, z, y, x, value)

    def for_each(body, start=0, stop=4):
        def step(j, carry):
            body(j)
            return carry

        lax.fori_loop(start, stop, step, 0)

    def prepare_off(j):
        transpose_inverse(OFF, j)
        transpose_slab(OFF, j)

    d_load.wait()
    for_each(prepare_off, 0, 1)
    pl.semaphore_wait(barrier, 5)
    for kind in (OFF, IN):
        for j in range(3):
            in_copy(kind, j).start()
    for_each(prepare_off, 1, 4)
    b_load.wait()
    first(OFF, 3)
    for_each(lambda j: transpose_inverse(IN, j))
    for_each(lambda j: transpose_slab(IN, j), 0, 2)
    for j in range(3):
        in_copy(OFF, j, True).wait_recv()
        first(OFF, j)
    for_each(lambda j: transpose_slab(IN, j), 2, 4)
    first(IN, 3)
    for j in range(3):
        in_copy(IN, j, True).wait_recv()
        first(IN, j)

    for it in range(ITERS - 2):

        def store(t, z, y, x, value, it=it):
            field[it + 1, t + 1, z, y, x] = value

        def step_off(j, it=it, store=store):
            finish_off(it, j, store)
            halo_copy(OFF, it + 1, j).start()

        def step_in(pair, it=it, store=store):
            steps = (2 * pair, 2 * pair + 1)
            finish_in(it, steps, (store, store))
            for j in steps:
                halo_copy(IN, it + 1, j).start()

        for_each(lambda pair: interior(it, pair), 0, 2)
        if it == 0:
            for_each(lambda j: transpose_slab(IN, j), 4, 4)
        for_each(step_off)
        for_each(step_in, 0, 2)

    def out_copy(kind, j):
        peer, t = slab(j), times[kind]
        return pltpu.make_async_remote_copy(
            src_ref=last.at[t, :, peer],
            dst_ref=gathered.at[t, :, :, part(g), :],
            send_sem=out_send.at[kind, j],
            recv_sem=out_recv.at[kind, j],
            device_id={"group": peer},
            device_id_type=MESH,
        )

    def store_last(t, z, y, x, value):
        last[t, z, y, x] = value

    def store_own(t, z, y, x, value):
        gathered[t, z, x, part(g), :] = value

    it = ITERS - 2

    def last_off(j):
        finish_off(it, j, store_last)
        out_copy(OFF, j).start()

    for_each(lambda pair: interior(it, pair), 0, 2)
    finish_in(it, (0, 1), (store_last, store_last))
    for j in (0, 1):
        out_copy(IN, j).start()
    finish_in(it, (2, 3), (store_last, store_own))
    out_copy(IN, 2).start()
    for_each(last_off, 0, 3)
    finish_off(it, 3, store_own)

    for load in p_loads:
        load.wait()
    for j in range(3):
        out_copy(IN, j).wait_recv()
    for z, x in sites:
        fine[z, x] = dot(gathered[times[IN], z, x], pro_in[z, x]).astype(BF16)
    for j in range(3):
        out_copy(OFF, j).wait_recv()

    for kind in (OFF, IN):
        for j in range(3):
            in_copy(kind, j).wait_send()
            out_copy(kind, j).wait_send()
        for k in range(ITERS - 1):
            for_each(lambda j: halo_copy(kind, k, j).wait_send())


def write_kernel(coarse, fine, pro_off, c_hbm, f_hbm, fine_off, sem):
    core = lax.rem(lax.axis_index("owner"), 2)
    copies = [
        pltpu.make_async_copy(coarse, c_hbm.at[:, :, 0], sem.at[0]),
        pltpu.make_async_copy(fine, f_hbm.at[1 - core, :, 0], sem.at[1]),
    ]
    for copy in copies:
        copy.start()
    for z in range(2):
        for x in range(4):
            fine_off[z, x] = dot(coarse[core, z, x], pro_off[z, x]).astype(BF16)
        copy = pltpu.make_async_copy(fine_off.at[z], f_hbm.at[core, z, 0], sem.at[2 + z])
        copy.start()
        copies.append(copy)
    for copy in copies:
        copy.wait()


def on_device(right_side, hops, diag_inverse, prolongator):
    vmem, dma = pltpu.VMEM, pltpu.SemaphoreType.DMA
    width = prolongator.shape[-1]
    parts = pl.pallas_call(
        kernel,
        out_shape=(
            vmem((2, 2, 4, C, C), BF16),
            vmem((2, 4, C, width), BF16),
            vmem((2, 4, C, width), BF16),
        ),
        in_specs=[pl.BlockSpec(memory_space=pl.ANY)] * 4,
        out_specs=(pl.BlockSpec(memory_space=vmem),) * 3,
        scratch_shapes=[
            vmem((8, 2, 2, 4, 4, C, C), BF16),
            vmem((2, 2, 4, 4, DIRS * C, C), BF16),
            vmem((2, 2, 4, 4, C, C), BF16),
            vmem((2, 2, 4, 4, PART, C), BF16),
            vmem((ITERS - 1, 4, 2, 4, 4, PART, C), BF16),
            vmem((2, 2, 4, 4, PART, C), BF16),
            vmem((4, 8, PART, C), F32),
            vmem((2, 4, C, width), BF16),
            dma((2, 4, 2)),
            dma,
            dma((2,)),
            dma,
            dma((2, 3)),
            dma((2, 3)),
            dma((2, ITERS - 1, 4)),
            dma((2, ITERS - 1, 4)),
            dma((2, 3)),
            dma((2, 3)),
        ],
        compiler_params=pltpu.CompilerParams(
            collective_id=0, has_side_effects=True, vmem_limit_bytes=VMEM_LIMIT
        ),
        cost_estimate=pl.CostEstimate(
            flops=2 * 64 * 28 * C * C * PART, bytes_accessed=24 * 1024 * 1024, transcendentals=0
        ),
    )(right_side, hops, diag_inverse, prolongator)
    return pl.pallas_call(
        write_kernel,
        out_shape=(
            jax.ShapeDtypeStruct(right_side.shape, BF16),
            jax.ShapeDtypeStruct(prolongator.shape, BF16),
        ),
        in_specs=[pl.BlockSpec(memory_space=vmem)] * 3,
        out_specs=(pl.BlockSpec(memory_space=pl.ANY),) * 2,
        scratch_shapes=[vmem((2, 4, C, width), BF16), dma((4,))],
    )(*(pltpu.with_memory_space_constraint(array, vmem) for array in parts))


def solution(mesh):
    placed = (
        P("owner", None, "group", None, None, None),
        P(None, "owner", None, None, None, None, None),
        P("owner", None, None, None, None, None),
        P("owner", None, "group", None, None, None),
    )
    return jax.shard_map(
        on_device,
        mesh=mesh,
        in_specs=placed,
        out_specs=(
            P("owner", None, "group", None, None, None),
            P("owner", None, "group", None, None, None),
        ),
        check_vma=False,
    )
```

```python
import functools

import jax
import jax.numpy as jnp
from jax import lax
from jax.experimental import pallas as pl
from jax.experimental.pallas import tpu as pltpu
from jax.sharding import PartitionSpec as P

MESH = pl.DeviceIdType.MESH
ITERS = 4
C = 128
PART = 32
DIRS = 7
OFF, IN = 0, 1
VMEM_LIMIT = 56 * 1024 * 1024
F32 = jnp.float32
BF16 = jnp.bfloat16


def dot(left, right):
    return lax.dot_general(
        left, right, (((1,), (0,)), ((), ())), preferred_element_type=F32
    )


def offset_of(step):
    return lax.rem(2 + 3 * step + 3 * lax.div(step, 2) + 2 * lax.div(step, 3), 4)


MIRROR = (0, 2, 1)


def kernel(
    b_hbm, h_hbm, d_hbm, p_hbm, gathered, fine, pro_off,
    hs, ht, ds, rhs, field, last, acc, pro_in,
    h_sem, d_sem, p_sem, b_sem,
    in_send, in_recv, halo_send, halo_recv, out_send, out_recv,
):
    g = lax.axis_index("group")
    o = lax.axis_index("owner")
    core = lax.rem(o, 2)
    times = (core, 1 - core)

    def slab(j):
        return lax.rem(g + offset_of(j), 4)

    def part(index):
        return pl.ds(pl.multiple_of(index * PART, PART), PART)

    barrier = pltpu.get_barrier_semaphore()
    for k in (1, 31):
        pl.semaphore_signal(
            barrier, inc=1, device_id={"owner": lax.rem(o + k, 32)}, device_id_type=MESH
        )
    for k in (1, 2, 3):
        pl.semaphore_signal(
            barrier, inc=1, device_id={"group": lax.rem(g + k, 4)}, device_id_type=MESH
        )

    d_load = pltpu.make_async_copy(d_hbm, ds, d_sem)
    d_load.start()
    b_load = pltpu.make_async_copy(b_hbm.at[:, :, 0, :, part(g), :], rhs.at[:, :, g], b_sem)
    b_load.start()

    def h_load(kind, j, z):
        t, y = times[kind], slab(j)
        return pltpu.make_async_copy(
            h_hbm.at[:, t, z, y], hs.at[:, t, z, y], h_sem.at[kind, j, z]
        )

    for kind in (OFF, IN):

        def start_loads(j, carry, kind=kind):
            for z in range(2):
                h_load(kind, j, z).start()
            return carry

        lax.fori_loop(0, 4, start_loads, 0)
    p_loads = [
        pltpu.make_async_copy(p_hbm.at[times[IN], :, 0], pro_in, p_sem.at[IN]),
        pltpu.make_async_copy(p_hbm.at[times[OFF], :, 0], pro_off, p_sem.at[OFF]),
    ]
    for load in p_loads:
        load.start()

    def in_copy(kind, j, arrives=False):
        peer, t = slab(j), times[kind]
        return pltpu.make_async_remote_copy(
            src_ref=b_hbm.at[t, :, 0, :, part(peer), :],
            dst_ref=rhs.at[t, :, peer if arrives else g],
            send_sem=in_send.at[kind, j],
            recv_sem=in_recv.at[kind, j if arrives else MIRROR[j]],
            device_id={"group": peer},
            device_id_type=MESH,
        )

    def halo_copy(kind, it, j, arrives=False):
        t, y = times[kind], slab(j)
        return pltpu.make_async_remote_copy(
            src_ref=field.at[it, t + 1, :, y],
            dst_ref=field.at[it, 3 * t if arrives else 3 - 3 * t, :, y],
            send_sem=halo_send.at[kind, it, j],
            recv_sem=halo_recv.at[kind, it, j],
            device_id={"owner": lax.rem(o + 31 + 2 * t, 32)},
            device_id_type=MESH,
        )

    sites = [(z, x) for z in range(2) for x in range(4)]

    def transpose_slab(kind, j):
        t, y = times[kind], slab(j)
        inner, outer = 6 + t, 7 - t
        for z in range(2):
            h_load(kind, j, z).wait()
            for x in range(4):
                blocks = [hs[k, t, z, y, x] for k in range(4)]
                blocks.append(hs[4, t, z, y, x] + hs[5, t, z, y, x])
                blocks.append(hs[inner, t, z, y, x])
                blocks.append(hs[outer, t, z, y, x])
                for k, block in enumerate(blocks):
                    ht[t, z, y, x, k * C : (k + 1) * C, :] = block.T

    def transpose_inverse(kind, j):
        t, y = times[kind], slab(j)
        for z, x in sites:
            ds[t, z, y, x] = ds[t, z, y, x].T

    def first(kind, j):
        t, y = times[kind], slab(j)
        for z, x in sites:
            field[0, t + 1, z, y, x] = dot(rhs[t, z, y, x], ds[t, z, y, x]).astype(BF16)
        halo_copy(kind, 0, j).start()

    def near(it, t, z, y, x):
        return [
            field[it, t + 1, z, y, (x + 1) % 4],
            field[it, t + 1, z, y, (x + 3) % 4],
            field[it, t + 1, z, lax.rem(y + 1, 4), x],
            field[it, t + 1, z, lax.rem(y + 3, 4), x],
            field[it, t + 1, 1 - z, y, x],
            field[it, 2 - t, z, y, x],
        ]

    def interior(it, pair):
        t = times[OFF]
        for j in (2 * pair, 2 * pair + 1):
            y = slab(j)
            for q, (z, x) in enumerate(sites):
                total = dot(
                    jnp.concatenate(near(it, t, z, y, x), axis=1), ht[t, z, y, x, : 6 * C, :]
                )
                acc[j, q] = rhs[t, z, y, x].astype(F32) - total

    def finish_off(it, j, store):
        t, y = times[OFF], slab(j)
        halo_copy(OFF, it, j, True).wait_recv()
        remainders = [
            acc[j, q] - dot(field[it, 3 * t, z, y, x], ht[t, z, y, x, 6 * C :, :])
            for q, (z, x) in enumerate(sites)
        ]
        for remainder, (z, x) in zip(remainders, sites):
            value = dot(remainder.astype(BF16), ds[t, z, y, x]).astype(BF16)
            store(t, z, y, x, value)

    def finish_in(it, steps, stores):
        t = times[IN]
        for j in steps:
            halo_copy(IN, it, j, True).wait_recv()
        places = [(k, slab(j), z, x) for k, j in enumerate(steps) for z, x in sites]
        remainders = [
            rhs[t, z, y, x].astype(F32)
            - dot(
                jnp.concatenate(near(it, t, z, y, x) + [field[it, 3 * t, z, y, x]], axis=1),
                ht[t, z, y, x],
            )
            for k, y, z, x in places
        ]
        for remainder, (k, y, z, x) in zip(remainders, places):
            value = dot(remainder.astype(BF16), ds[t, z, y, x]).astype(BF16)
            stores[k](t, z, y, x, value)

    def for_each(body, start=0, stop=4):
        def step(j, carry):
            body(j)
            return carry

        lax.fori_loop(start, stop, step, 0)

    def prepare_off(j):
        transpose_inverse(OFF, j)
        transpose_slab(OFF, j)

    d_load.wait()
    for_each(prepare_off, 0, 1)
    pl.semaphore_wait(barrier, 5)
    for j in range(3):
        in_copy(OFF, j).start()
    for_each(prepare_off, 1, 3)
    for j in range(3):
        in_copy(IN, j).start()
    for_each(prepare_off, 3, 4)
    b_load.wait()
    first(OFF, 3)
    for_each(lambda j: transpose_inverse(IN, j))
    for_each(lambda j: transpose_slab(IN, j), 0, 2)
    for j in range(3):
        in_copy(OFF, j, True).wait_recv()
        first(OFF, j)
    for_each(lambda j: transpose_slab(IN, j), 2, 4)
    first(IN, 3)
    for j in range(3):
        in_copy(IN, j, True).wait_recv()
        first(IN, j)

    for it in range(ITERS - 2):

        def store(t, z, y, x, value, it=it):
            field[it + 1, t + 1, z, y, x] = value

        def step_off(j, it=it, store=store):
            finish_off(it, j, store)
            halo_copy(OFF, it + 1, j).start()

        def step_in(pair, it=it, store=store):
            steps = (2 * pair, 2 * pair + 1)
            finish_in(it, steps, (store, store))
            for j in steps:
                halo_copy(IN, it + 1, j).start()

        for_each(lambda pair: interior(it, pair), 0, 2)
        if it == 0:
            for_each(lambda j: transpose_slab(IN, j), 4, 4)
        for_each(step_off)
        for_each(step_in, 0, 2)

    def out_copy(kind, j):
        peer, t = slab(j), times[kind]
        return pltpu.make_async_remote_copy(
            src_ref=last.at[t, :, peer],
            dst_ref=gathered.at[t, :, :, part(g), :],
            send_sem=out_send.at[kind, j],
            recv_sem=out_recv.at[kind, j],
            device_id={"group": peer},
            device_id_type=MESH,
        )

    def store_last(t, z, y, x, value):
        last[t, z, y, x] = value

    def store_own(t, z, y, x, value):
        gathered[t, z, x, part(g), :] = value

    it = ITERS - 2

    def last_off(j):
        finish_off(it, j, store_last)
        out_copy(OFF, j).start()

    for_each(lambda pair: interior(it, pair), 0, 2)
    finish_in(it, (0, 1), (store_last, store_last))
    for j in (0, 1):
        out_copy(IN, j).start()
    finish_in(it, (2, 3), (store_last, store_own))
    out_copy(IN, 2).start()
    for_each(last_off, 0, 3)
    finish_off(it, 3, store_own)

    for load in p_loads:
        load.wait()
    for j in range(3):
        out_copy(IN, j).wait_recv()
    for z, x in sites:
        fine[z, x] = dot(gathered[times[IN], z, x], pro_in[z, x]).astype(BF16)
    for kind in (OFF, IN):
        for j in range(3):
            in_copy(kind, j).wait_send()
        for k in range(ITERS - 1):
            for_each(lambda j: halo_copy(kind, k, j).wait_send())
    for j in range(3):
        out_copy(IN, j).wait_send()
    for j in range(3):
        out_copy(OFF, j).wait_send()
    for j in range(3):
        out_copy(OFF, j).wait_recv()


def write_kernel(coarse, fine, pro_off, c_hbm, f_hbm, fine_off, sem):
    core = lax.rem(lax.axis_index("owner"), 2)
    copies = [
        pltpu.make_async_copy(coarse, c_hbm.at[:, :, 0], sem.at[0]),
        pltpu.make_async_copy(fine, f_hbm.at[1 - core, :, 0], sem.at[1]),
    ]
    for copy in copies:
        copy.start()
    for z in range(2):
        for x in range(4):
            fine_off[z, x] = dot(coarse[core, z, x], pro_off[z, x]).astype(BF16)
        copy = pltpu.make_async_copy(fine_off.at[z], f_hbm.at[core, z, 0], sem.at[2 + z])
        copy.start()
        copies.append(copy)
    for copy in copies:
        copy.wait()


def on_device(right_side, hops, diag_inverse, prolongator):
    vmem, dma = pltpu.VMEM, pltpu.SemaphoreType.DMA
    width = prolongator.shape[-1]
    parts = pl.pallas_call(
        kernel,
        out_shape=(
            vmem((2, 2, 4, C, C), BF16),
            vmem((2, 4, C, width), BF16),
            vmem((2, 4, C, width), BF16),
        ),
        in_specs=[pl.BlockSpec(memory_space=pl.ANY)] * 4,
        out_specs=(pl.BlockSpec(memory_space=vmem),) * 3,
        scratch_shapes=[
            vmem((8, 2, 2, 4, 4, C, C), BF16),
            vmem((2, 2, 4, 4, DIRS * C, C), BF16),
            vmem((2, 2, 4, 4, C, C), BF16),
            vmem((2, 2, 4, 4, PART, C), BF16),
            vmem((ITERS - 1, 4, 2, 4, 4, PART, C), BF16),
            vmem((2, 2, 4, 4, PART, C), BF16),
            vmem((4, 8, PART, C), F32),
            vmem((2, 4, C, width), BF16),
            dma((2, 4, 2)),
            dma,
            dma((2,)),
            dma,
            dma((2, 3)),
            dma((2, 3)),
            dma((2, ITERS - 1, 4)),
            dma((2, ITERS - 1, 4)),
            dma((2, 3)),
            dma((2, 3)),
        ],
        compiler_params=pltpu.CompilerParams(
            collective_id=0, has_side_effects=True, vmem_limit_bytes=VMEM_LIMIT
        ),
        cost_estimate=pl.CostEstimate(
            flops=2 * 64 * 28 * C * C * PART, bytes_accessed=24 * 1024 * 1024, transcendentals=0
        ),
    )(right_side, hops, diag_inverse, prolongator)
    return pl.pallas_call(
        write_kernel,
        out_shape=(
            jax.ShapeDtypeStruct(right_side.shape, BF16),
            jax.ShapeDtypeStruct(prolongator.shape, BF16),
        ),
        in_specs=[pl.BlockSpec(memory_space=vmem)] * 3,
        out_specs=(pl.BlockSpec(memory_space=pl.ANY),) * 2,
        scratch_shapes=[vmem((2, 4, C, width), BF16), dma((4,))],
    )(*(pltpu.with_memory_space_constraint(array, vmem) for array in parts))


def solution(mesh):
    placed = (
        P("owner", None, "group", None, None, None),
        P(None, "owner", None, None, None, None, None),
        P("owner", None, None, None, None, None),
        P("owner", None, "group", None, None, None),
    )
    return jax.shard_map(
        on_device,
        mesh=mesh,
        in_specs=placed,
        out_specs=(
            P("owner", None, "group", None, None, None),
            P("owner", None, "group", None, None, None),
        ),
        check_vma=False,
    )
```

```python
import functools

import jax
import jax.numpy as jnp
from jax import lax
from jax.experimental import pallas as pl
from jax.experimental.pallas import tpu as pltpu
from jax.sharding import PartitionSpec as P

MESH = pl.DeviceIdType.MESH
ITERS = 4
C = 128
PART = 32
DIRS = 7
OFF, IN = 0, 1
VMEM_LIMIT = 56 * 1024 * 1024
F32 = jnp.float32
BF16 = jnp.bfloat16


def dot(left, right):
    return lax.dot_general(
        left, right, (((1,), (0,)), ((), ())), preferred_element_type=F32
    )


def offset_of(step):
    return lax.rem(2 + 3 * step + 3 * lax.div(step, 2) + 2 * lax.div(step, 3), 4)


MIRROR = (0, 2, 1)


def kernel(
    b_hbm, h_hbm, d_hbm, p_hbm, gathered, fine, pro_off,
    hs, ht, ds, rhs, field, last, acc, pro_in,
    h_sem, d_sem, p_sem, b_sem,
    in_send, in_recv, halo_send, halo_recv, out_send, out_recv,
):
    g = lax.axis_index("group")
    o = lax.axis_index("owner")
    core = lax.rem(o, 2)
    times = (core, 1 - core)

    def slab(j):
        return lax.rem(g + offset_of(j), 4)

    def part(index):
        return pl.ds(pl.multiple_of(index * PART, PART), PART)

    barrier = pltpu.get_barrier_semaphore()
    for k in (1, 31):
        pl.semaphore_signal(
            barrier, inc=1, device_id={"owner": lax.rem(o + k, 32)}, device_id_type=MESH
        )
    for k in (1, 2, 3):
        pl.semaphore_signal(
            barrier, inc=1, device_id={"group": lax.rem(g + k, 4)}, device_id_type=MESH
        )

    d_load = pltpu.make_async_copy(d_hbm, ds, d_sem)
    d_load.start()
    b_load = pltpu.make_async_copy(b_hbm.at[:, :, 0, :, part(g), :], rhs.at[:, :, g], b_sem)
    b_load.start()

    def h_load(kind, j, z):
        t, y = times[kind], slab(j)
        return pltpu.make_async_copy(
            h_hbm.at[:, t, z, y], hs.at[:, t, z, y], h_sem.at[kind, j, z]
        )

    for kind in (OFF, IN):

        def start_loads(j, carry, kind=kind):
            for z in range(2):
                h_load(kind, j, z).start()
            return carry

        lax.fori_loop(0, 4, start_loads, 0)
    p_loads = [
        pltpu.make_async_copy(p_hbm.at[times[IN], :, 0], pro_in, p_sem.at[IN]),
        pltpu.make_async_copy(p_hbm.at[times[OFF], :, 0], pro_off, p_sem.at[OFF]),
    ]
    for load in p_loads:
        load.start()

    def in_copy(kind, j, arrives=False):
        peer, t = slab(j), times[kind]
        return pltpu.make_async_remote_copy(
            src_ref=b_hbm.at[t, :, 0, :, part(peer), :],
            dst_ref=rhs.at[t, :, peer if arrives else g],
            send_sem=in_send.at[kind, j],
            recv_sem=in_recv.at[kind, j if arrives else MIRROR[j]],
            device_id={"group": peer},
            device_id_type=MESH,
        )

    def halo_copy(kind, it, j, arrives=False):
        t, y = times[kind], slab(j)
        return pltpu.make_async_remote_copy(
            src_ref=field.at[it, t + 1, :, y],
            dst_ref=field.at[it, 3 * t if arrives else 3 - 3 * t, :, y],
            send_sem=halo_send.at[kind, it, j],
            recv_sem=halo_recv.at[kind, it, j],
            device_id={"owner": lax.rem(o + 31 + 2 * t, 32)},
            device_id_type=MESH,
        )

    sites = [(z, x) for z in range(2) for x in range(4)]

    def transpose_slab(kind, j):
        t, y = times[kind], slab(j)
        inner, outer = 6 + t, 7 - t
        for z in range(2):
            h_load(kind, j, z).wait()
            for x in range(4):
                blocks = [hs[k, t, z, y, x] for k in range(4)]
                blocks.append(hs[4, t, z, y, x] + hs[5, t, z, y, x])
                blocks.append(hs[inner, t, z, y, x])
                blocks.append(hs[outer, t, z, y, x])
                for k, block in enumerate(blocks):
                    ht[t, z, y, x, k * C : (k + 1) * C, :] = block.T

    def transpose_inverse(kind, j):
        t, y = times[kind], slab(j)
        for z, x in sites:
            ds[t, z, y, x] = ds[t, z, y, x].T

    def first(kind, j):
        t, y = times[kind], slab(j)
        for z, x in sites:
            field[0, t + 1, z, y, x] = dot(rhs[t, z, y, x], ds[t, z, y, x]).astype(BF16)
        halo_copy(kind, 0, j).start()

    def near(it, t, z, y, x):
        return [
            field[it, t + 1, z, y, (x + 1) % 4],
            field[it, t + 1, z, y, (x + 3) % 4],
            field[it, t + 1, z, lax.rem(y + 1, 4), x],
            field[it, t + 1, z, lax.rem(y + 3, 4), x],
            field[it, t + 1, 1 - z, y, x],
            field[it, 2 - t, z, y, x],
        ]

    def interior(it, pair):
        t = times[OFF]
        for j in (2 * pair, 2 * pair + 1):
            y = slab(j)
            for q, (z, x) in enumerate(sites):
                total = dot(
                    jnp.concatenate(near(it, t, z, y, x), axis=1), ht[t, z, y, x, : 6 * C, :]
                )
                acc[j, q] = rhs[t, z, y, x].astype(F32) - total

    def finish_off(it, j, store):
        t, y = times[OFF], slab(j)
        halo_copy(OFF, it, j, True).wait_recv()
        remainders = [
            acc[j, q] - dot(field[it, 3 * t, z, y, x], ht[t, z, y, x, 6 * C :, :])
            for q, (z, x) in enumerate(sites)
        ]
        for remainder, (z, x) in zip(remainders, sites):
            value = dot(remainder.astype(BF16), ds[t, z, y, x]).astype(BF16)
            store(t, z, y, x, value)

    def finish_in(it, steps, stores):
        t = times[IN]
        for j in steps:
            halo_copy(IN, it, j, True).wait_recv()
        places = [(k, slab(j), z, x) for k, j in enumerate(steps) for z, x in sites]
        remainders = [
            rhs[t, z, y, x].astype(F32)
            - dot(
                jnp.concatenate(near(it, t, z, y, x) + [field[it, 3 * t, z, y, x]], axis=1),
                ht[t, z, y, x],
            )
            for k, y, z, x in places
        ]
        for remainder, (k, y, z, x) in zip(remainders, places):
            value = dot(remainder.astype(BF16), ds[t, z, y, x]).astype(BF16)
            stores[k](t, z, y, x, value)

    def for_each(body, start=0, stop=4):
        def step(j, carry):
            body(j)
            return carry

        lax.fori_loop(start, stop, step, 0)

    def prepare_off(j):
        transpose_inverse(OFF, j)
        transpose_slab(OFF, j)

    d_load.wait()
    for_each(prepare_off, 0, 1)
    pl.semaphore_wait(barrier, 5)
    for j in range(3):
        in_copy(OFF, j).start()
    for_each(prepare_off, 1, 3)
    for j in range(3):
        in_copy(IN, j).start()
    for_each(prepare_off, 3, 4)
    b_load.wait()
    first(OFF, 3)
    for_each(lambda j: transpose_inverse(IN, j))
    for_each(lambda j: transpose_slab(IN, j), 0, 2)
    for j in range(3):
        in_copy(OFF, j, True).wait_recv()
        first(OFF, j)
    for_each(lambda j: transpose_slab(IN, j), 2, 4)
    first(IN, 3)
    for j in range(3):
        in_copy(IN, j, True).wait_recv()
        first(IN, j)

    for it in range(ITERS - 2):

        def store(t, z, y, x, value, it=it):
            field[it + 1, t + 1, z, y, x] = value

        def step_off(j, it=it, store=store):
            finish_off(it, j, store)
            halo_copy(OFF, it + 1, j).start()

        def step_in(pair, it=it, store=store):
            steps = (2 * pair, 2 * pair + 1)
            finish_in(it, steps, (store, store))
            for j in steps:
                halo_copy(IN, it + 1, j).start()

        for_each(lambda pair: interior(it, pair), 0, 2)
        for_each(step_in, 0, 2)
        for_each(step_off)

    def out_copy(kind, j):
        peer, t = slab(j), times[kind]
        return pltpu.make_async_remote_copy(
            src_ref=last.at[t, :, peer],
            dst_ref=gathered.at[t, :, :, part(g), :],
            send_sem=out_send.at[kind, j],
            recv_sem=out_recv.at[kind, j],
            device_id={"group": peer},
            device_id_type=MESH,
        )

    def store_last(t, z, y, x, value):
        last[t, z, y, x] = value

    def store_own(t, z, y, x, value):
        gathered[t, z, x, part(g), :] = value

    it = ITERS - 2

    def last_off(j):
        finish_off(it, j, store_last)
        out_copy(OFF, j).start()

    for_each(lambda pair: interior(it, pair), 0, 2)
    finish_in(it, (0, 1), (store_last, store_last))
    for j in (0, 1):
        out_copy(IN, j).start()
    finish_in(it, (2, 3), (store_last, store_own))
    out_copy(IN, 2).start()
    for_each(last_off, 0, 3)
    finish_off(it, 3, store_own)

    for load in p_loads:
        load.wait()
    for j in range(3):
        out_copy(IN, j).wait_recv()
    for z, x in sites:
        fine[z, x] = dot(gathered[times[IN], z, x], pro_in[z, x]).astype(BF16)
    for kind in (OFF, IN):
        for j in range(3):
            in_copy(kind, j).wait_send()
        for k in range(ITERS - 1):
            for_each(lambda j: halo_copy(kind, k, j).wait_send())
    for j in range(3):
        out_copy(IN, j).wait_send()
    for j in range(3):
        out_copy(OFF, j).wait_send()
    for j in range(3):
        out_copy(OFF, j).wait_recv()


def write_kernel(coarse, fine, pro_off, c_hbm, f_hbm, fine_off, sem):
    core = lax.rem(lax.axis_index("owner"), 2)
    copies = [
        pltpu.make_async_copy(coarse, c_hbm.at[:, :, 0], sem.at[0]),
        pltpu.make_async_copy(fine, f_hbm.at[1 - core, :, 0], sem.at[1]),
    ]
    for copy in copies:
        copy.start()
    for z in range(2):
        for x in range(4):
            fine_off[z, x] = dot(coarse[core, z, x], pro_off[z, x]).astype(BF16)
            if x % 2:
                pair = pl.ds(x - 1, 2)
                copy = pltpu.make_async_copy(
                    fine_off.at[z, pair], f_hbm.at[core, z, 0, pair], sem.at[2 + 2 * z + x // 2]
                )
                copy.start()
                copies.append(copy)
    for copy in copies:
        copy.wait()


def on_device(right_side, hops, diag_inverse, prolongator):
    vmem, dma = pltpu.VMEM, pltpu.SemaphoreType.DMA
    width = prolongator.shape[-1]
    parts = pl.pallas_call(
        kernel,
        out_shape=(
            vmem((2, 2, 4, C, C), BF16),
            vmem((2, 4, C, width), BF16),
            vmem((2, 4, C, width), BF16),
        ),
        in_specs=[pl.BlockSpec(memory_space=pl.ANY)] * 4,
        out_specs=(pl.BlockSpec(memory_space=vmem),) * 3,
        scratch_shapes=[
            vmem((8, 2, 2, 4, 4, C, C), BF16),
            vmem((2, 2, 4, 4, DIRS * C, C), BF16),
            vmem((2, 2, 4, 4, C, C), BF16),
            vmem((2, 2, 4, 4, PART, C), BF16),
            vmem((ITERS - 1, 4, 2, 4, 4, PART, C), BF16),
            vmem((2, 2, 4, 4, PART, C), BF16),
            vmem((4, 8, PART, C), F32),
            vmem((2, 4, C, width), BF16),
            dma((2, 4, 2)),
            dma,
            dma((2,)),
            dma,
            dma((2, 3)),
            dma((2, 3)),
            dma((2, ITERS - 1, 4)),
            dma((2, ITERS - 1, 4)),
            dma((2, 3)),
            dma((2, 3)),
        ],
        compiler_params=pltpu.CompilerParams(
            collective_id=0, has_side_effects=True, vmem_limit_bytes=VMEM_LIMIT
        ),
        cost_estimate=pl.CostEstimate(
            flops=2 * 64 * 28 * C * C * PART, bytes_accessed=24 * 1024 * 1024, transcendentals=0
        ),
    )(right_side, hops, diag_inverse, prolongator)
    return pl.pallas_call(
        write_kernel,
        out_shape=(
            jax.ShapeDtypeStruct(right_side.shape, BF16),
            jax.ShapeDtypeStruct(prolongator.shape, BF16),
        ),
        in_specs=[pl.BlockSpec(memory_space=vmem)] * 3,
        out_specs=(pl.BlockSpec(memory_space=pl.ANY),) * 2,
        scratch_shapes=[vmem((2, 4, C, width), BF16), dma((6,))],
    )(*(pltpu.with_memory_space_constraint(array, vmem) for array in parts))


def solution(mesh):
    placed = (
        P("owner", None, "group", None, None, None),
        P(None, "owner", None, None, None, None, None),
        P("owner", None, None, None, None, None),
        P("owner", None, "group", None, None, None),
    )
    return jax.shard_map(
        on_device,
        mesh=mesh,
        in_specs=placed,
        out_specs=(
            P("owner", None, "group", None, None, None),
            P("owner", None, "group", None, None, None),
        ),
        check_vma=False,
    )
```
